512 devices in a mesh: prow: 32 (over z, core), pcol: 16 (over y, x).
Axes of the slice: x: 4, y: 4, z: 16, core: 2. Of those that a mesh axis runs over, the one named last changes fastest.
Arguments:
- rhs: float32 [4, 32, 16, 64, 128], P(None, 'prow', 'pcol'), may hold values from -6 to 6
- l_inverse: float32 [4, 32, 16, 128, 128], P(None, 'prow', 'pcol'), may hold values from -0.15 to 1.5
- u_inverse: float32 [4, 32, 16, 128, 128], P(None, 'prow', 'pcol'), may hold values from -0.15 to 1.5
- l_tiles: float32 [3, 32, 16, 16, 64, 128], P(None, 'prow', 'pcol'), may hold values from -0.125 to 0.125
- l_source: int32 [3, 32, 16, 16], P(None, 'prow', 'pcol'), may hold values from 0 to 31, as said below
- l_target: int32 [3, 32, 16, 16], P(None, 'prow', 'pcol'), may hold values from 0 to 15, as said below
- l_rows: int32 [3, 32, 16, 16, 64], P(None, 'prow', 'pcol'), may hold values from 0 to 127, as said below
- u_tiles: float32 [3, 32, 16, 16, 64, 128], P(None, 'prow', 'pcol'), may hold values from -0.125 to 0.125
- u_source: int32 [3, 32, 16, 16], P(None, 'prow', 'pcol'), may hold values from 0 to 31, as said below
- u_target: int32 [3, 32, 16, 16], P(None, 'prow', 'pcol'), may hold values from 0 to 15, as said below
- u_cols: int32 [3, 32, 16, 16, 64], P(None, 'prow', 'pcol'), may hold values from 0 to 127, as said below
Outputs:
- solution: float32 [4, 32, 16, 64, 128], P(None, 'prow', 'pcol')
The draws below stay inside these ranges and needn't reach their ends.
Inputs may be any that keep to these rules, and one draw needn't show every extreme that they name: Within one device and level the 16 pairs (l_source, l_target) are distinct; over all devices each pair of a source process row and a target process column occurs 16 times a level. `l_target`: see l_source. `l_rows`: distinct and increasing within a tile. The structure of U is that of L transposed: U tile k of a level on device (r, c) belongs to L tile k of that level on device (u_source, u_target), whose l_source is r and l_target is c. `u_target`: see u_source. `u_cols`: equal to the l_rows of the L tile that the U tile belongs to.
All inputs are finite; a program needn't handle non-finite values.
Results may differ from the reference program's by a relative error of at most 0.0001.
Values sent between devices are 32-bit elements; how exact they have to be, the bound alone decides.
No kernel may reach another device: no remote copies, remote signals or barrier semaphores. Data moves between devices by JAX's collectives and lax.ppermute only.
A program may use at most 64 MiB of HBM per device.

```python
import jax
import jax.numpy as jnp
from jax import lax

BLOCK = 128
TILE_ROWS = 64
NRHS = 64
LEVELS = 4
TILES_DEV = 16
PROC_ROWS = 32
PROC_COLS = 16


def tile_structure(key):
    total = PROC_ROWS * PROC_COLS
    level_keys = jax.random.split(key, LEVELS - 1)

    def one_level(level_key):
        order_key, rows_key = jax.random.split(level_key)
        order = jax.random.permutation(order_key, total).astype(jnp.int32)
        place = jnp.zeros((total,), jnp.int32).at[order].set(jnp.arange(total, dtype=jnp.int32))
        offsets = jnp.arange(TILES_DEV, dtype=jnp.int32)
        partner = order[(place[:, None] + offsets[None, :]) % total]
        owner = order[(place[:, None] - offsets[None, :]) % total]
        row_keys = jax.random.split(rows_key, total * TILES_DEV)
        subsets = jax.vmap(lambda sub_key: jnp.sort(jax.random.permutation(sub_key, BLOCK)[:TILE_ROWS]))(row_keys)
        subsets = subsets.astype(jnp.int32).reshape(total, TILES_DEV, TILE_ROWS)
        columns = subsets[owner, offsets[None, :]]
        return (partner, owner, subsets, columns)
    partner, owner, subsets, columns = jax.vmap(one_level)(level_keys)
    shape = (LEVELS - 1, PROC_ROWS, PROC_COLS, TILES_DEV)
    return ((partner // PROC_COLS).reshape(shape), (partner % PROC_COLS).reshape(shape), subsets.reshape(shape + (TILE_ROWS,)), (owner // PROC_COLS).reshape(shape), (owner % PROC_COLS).reshape(shape), columns.reshape(shape + (TILE_ROWS,)))


def triangle_inverse(key, upper, diag_low, diag_high, off_reach):
    diag_key, off_key = jax.random.split(key)
    shape = (LEVELS, PROC_ROWS, PROC_COLS, BLOCK, BLOCK)
    row_pos = lax.broadcasted_iota(jnp.int32, (BLOCK, BLOCK), 0)
    col_pos = lax.broadcasted_iota(jnp.int32, (BLOCK, BLOCK), 1)
    if upper:
        keep = (col_pos > row_pos).astype(jnp.float32)
    else:
        keep = (col_pos < row_pos).astype(jnp.float32)
    diagonal = (row_pos == col_pos).astype(jnp.float32)
    diag_values = jax.random.uniform(diag_key, shape, jnp.float32, diag_low, diag_high)
    off_values = jax.random.uniform(off_key, shape, jnp.float32, -off_reach, off_reach)
    return diag_values * diagonal + off_values * keep


def draw_l_inverse(key, part):
    key = jax.random.fold_in(key, 11)
    return triangle_inverse(key, False, 0.7, 1.4, 0.12)


def draw_u_inverse(key, part):
    key = jax.random.fold_in(key, 12)
    return triangle_inverse(key, True, 0.7, 1.4, 0.12)


def draw_l_source(key, part):
    tables = tile_structure(key)
    return tables[0]


def draw_l_target(key, part):
    tables = tile_structure(key)
    return tables[1]


def draw_l_rows(key, part):
    tables = tile_structure(key)
    return tables[2]


def draw_u_source(key, part):
    tables = tile_structure(key)
    return tables[3]


def draw_u_target(key, part):
    tables = tile_structure(key)
    return tables[4]


def draw_u_cols(key, part):
    tables = tile_structure(key)
    return tables[5]


def levels(own_key, shape, shards, least, largest):
    def one(axis_at, blocks):
        steps = jax.random.uniform(jax.random.fold_in(jax.random.fold_in(own_key, 6), axis_at), (blocks,), jnp.float32, least / len(shards), largest / len(shards))
        return jnp.repeat(jnp.exp(steps), shape[axis_at] // blocks).reshape((-1,) + (1,) * (len(shape) - axis_at - 1))

    loudness = one(*shards[0])
    for cut in shards[1:]:
        loudness = loudness * one(*cut)
    return loudness


def bell_draw(stream_key, shape, scale, reach, shards=(), kind=jnp.bfloat16):
    values = jax.random.normal(stream_key, shape, jnp.float32) * scale
    if len(shards) > 0:
        values = levels(stream_key, shape, shards, -0.22, 0.18) * values
    return jnp.clip(values, min=-reach, max=reach).astype(kind)


def setup_inputs(seed: int = 0) -> dict:
    key_list = jax.random.split(jax.random.key(seed), 12)
    rhs = bell_draw(key_list[0], (LEVELS, PROC_ROWS, PROC_COLS, NRHS, BLOCK), 1.0, 6.0, ((1, 32), (2, 16)), jnp.float32)
    l_inverse = draw_l_inverse(jax.random.fold_in(key_list[11], 71), 0)
    u_inverse = draw_u_inverse(jax.random.fold_in(key_list[11], 71), 0)
    l_tiles = bell_draw(key_list[3], (LEVELS - 1, PROC_ROWS, PROC_COLS, TILES_DEV, TILE_ROWS, BLOCK), (2 * TILE_ROWS * TILES_DEV) ** -0.5, 0.125, ((1, 32), (2, 16)), jnp.float32)
    l_source = draw_l_source(jax.random.fold_in(key_list[11], 71), 0)
    l_target = draw_l_target(jax.random.fold_in(key_list[11], 71), 0)
    l_rows = draw_l_rows(jax.random.fold_in(key_list[11], 71), 0)
    u_tiles = bell_draw(key_list[7], (LEVELS - 1, PROC_ROWS, PROC_COLS, TILES_DEV, TILE_ROWS, BLOCK), (2 * TILE_ROWS * TILES_DEV) ** -0.5, 0.125, ((1, 32), (2, 16)), jnp.float32)
    u_source = draw_u_source(jax.random.fold_in(key_list[11], 71), 0)
    u_target = draw_u_target(jax.random.fold_in(key_list[11], 71), 0)
    u_cols = draw_u_cols(jax.random.fold_in(key_list[11], 71), 0)
    return dict(rhs=rhs, l_inverse=l_inverse, u_inverse=u_inverse, l_tiles=l_tiles, l_source=l_source, l_target=l_target, l_rows=l_rows, u_tiles=u_tiles, u_source=u_source, u_target=u_target, u_cols=u_cols)


def apply_inverse(vectors, inverse):
    return jnp.einsum('pqnj,pqij->pqni', vectors, inverse, precision=lax.Precision.HIGHEST)


def reference(rhs, l_inverse, u_inverse, l_tiles, l_source, l_target, l_rows, u_tiles, u_source, u_target, u_cols):
    column_ids = jnp.arange(PROC_COLS, dtype=jnp.int32)[None, :, None]
    row_ids = jnp.arange(PROC_ROWS, dtype=jnp.int32)[:, None, None, None]
    solved = apply_inverse(rhs[0], l_inverse[0])
    forward = [solved]
    for level_index in range(1, LEVELS):
        section = level_index - 1
        blocks = solved[l_source[section], column_ids]
        products = jnp.einsum('pqtnb,pqtrb->pqtnr', blocks, l_tiles[section], precision=lax.Precision.HIGHEST)
        flat_index = (l_target[section][..., None] * BLOCK + l_rows[section]).astype(jnp.int32)
        rows_all = jnp.broadcast_to(row_ids, flat_index.shape).astype(jnp.int32)
        lower = jnp.zeros((PROC_ROWS, NRHS, PROC_COLS * BLOCK), jnp.float32)
        lower = lower.at[rows_all, :, flat_index].add(jnp.transpose(products, (0, 1, 2, 4, 3)))
        lower = jnp.transpose(lower.reshape(PROC_ROWS, NRHS, PROC_COLS, BLOCK), (0, 2, 1, 3))
        solved = apply_inverse(rhs[level_index] - lower, l_inverse[level_index])
        forward.append(solved)
    slot_ids = jnp.arange(PROC_COLS, dtype=jnp.int32)
    current = apply_inverse(forward[LEVELS - 1], u_inverse[LEVELS - 1])
    result = [current]
    for level_index in range(LEVELS - 2, -1, -1):
        blocks = current[u_source[level_index], column_ids]
        picked = jnp.take_along_axis(blocks, u_cols[level_index][:, :, :, None, :], axis=4)
        products = jnp.einsum('pqtnr,pqtrb->pqtnb', picked, u_tiles[level_index], precision=lax.Precision.HIGHEST)
        onehot = (u_target[level_index][..., None] == slot_ids).astype(jnp.float32)
        upper = jnp.einsum('pqtnb,pqtc->pcnb', products, onehot, precision=lax.Precision.HIGHEST)
        current = apply_inverse(forward[level_index] - upper, u_inverse[level_index])
        result.append(current)
    return jnp.stack(result[::-1])
```

```python
import jax
import jax.numpy as jnp
from jax import lax
from jax.experimental import pallas as pl
from jax.experimental.pallas import tpu as pltpu
from jax.sharding import PartitionSpec as P

F32 = jnp.float32
BF16 = jnp.bfloat16
VMEM_LIMIT = 48 * 1024 * 1024


def dot_nt(a, b):
    return lax.dot_general(a, b, (((1,), (1,)), ((), ())), preferred_element_type=F32)


def dot_nn(a, b):
    return lax.dot_general(a, b, (((1,), (0,)), ((), ())), preferred_element_type=F32)


def split(x):
    high = x.astype(BF16)
    low = (x - high.astype(F32)).astype(BF16)
    return jnp.concatenate([high, low], axis=0)


def fold(x):
    half = x.shape[0] // 2
    return x[:half] + x[half:]


def apply_inverse(vectors, inverse):
    size = inverse.shape[0]
    out = fold(dot_nt(split(vectors), split(inverse)))
    return out[:, :size] + out[:, size:]


def structure_matrix(rows):
    positions = lax.broadcasted_iota(jnp.int32, (128, rows.shape[1]), 0)
    return jnp.where(positions == rows, 1.0, 0.0).astype(BF16)


def products_kernel(transposed, offset, source_ref, target_ref, rows_ref, blocks_ref, own_ref, oth_ref, out_ref, parts_ref):
    tiles = own_ref.shape[0]
    for first in range(0, 2 * tiles, 8):
        group = range(first, first + 8)
        held = []
        for t in group:
            block = split(blocks_ref[source_ref[offset + t]])
            tile = split((own_ref if t < tiles else oth_ref)[t % tiles])
            places = structure_matrix(rows_ref[t : t + 1, :])
            if transposed:
                held.append((fold(dot_nt(block, tile)), places))
            else:
                held.append((dot_nn(block, places).astype(BF16), tile))
        for t, (left, right) in zip(group, held):
            if transposed:
                parts_ref[t] = fold(dot_nt(split(left), right))
            else:
                parts_ref[t] = fold(dot_nn(left, right))
    out_ref[...] = jnp.zeros_like(out_ref)
    for t in range(2 * tiles):
        out_ref[target_ref[offset + t], t // tiles] += parts_ref[t]


def products(transposed, offset, level, oth_level, source, target, rows, blocks, own, oth):
    tiles = own.shape[1]
    cols, half, width = 16, blocks.shape[1], blocks.shape[2]
    spec = lambda at: pl.BlockSpec((None,) + own.shape[1:], lambda i: (at, 0, 0, 0))
    smem = pl.BlockSpec(memory_space=pltpu.SMEM)
    flops = 2 * tiles * 2 * 2 * (2 * half) * 128 * 128
    return pl.pallas_call(
        lambda *refs: products_kernel(transposed, offset, *refs),
        grid=(1,),
        out_shape=jax.ShapeDtypeStruct((cols, 2, half, width), F32),
        in_specs=[
            smem,
            smem,
            pl.BlockSpec((None,) + rows.shape[1:], lambda i: (offset // (2 * tiles), 0, 0)),
            pl.BlockSpec(blocks.shape, lambda i: (0, 0, 0)),
            spec(level),
            spec(oth_level),
        ],
        out_specs=pl.BlockSpec((cols, 2, half, width), lambda i: (0, 0, 0, 0)),
        scratch_shapes=[pltpu.VMEM((2 * tiles, half, width), F32)],
        compiler_params=pltpu.CompilerParams(vmem_limit_bytes=VMEM_LIMIT),
        cost_estimate=pl.CostEstimate(flops=flops, bytes_accessed=2 << 20, transcendentals=0),
    )(source, target, rows, blocks, own, oth)


def solve_kernel(then_upper, parts_ref, start_own_ref, start_oth_ref, own_ref, oth_ref, *rest):
    if then_upper:
        up_own_ref, up_oth_ref, mid_ref, out_ref = rest
    else:
        (out_ref,) = rest
    total = parts_ref[0]
    for k in range(1, parts_ref.shape[0]):
        total = total + parts_ref[k]
    for s, (start_ref, inv_ref) in enumerate(((start_own_ref, own_ref), (start_oth_ref, oth_ref))):
        value = apply_inverse(start_ref[...] - total[s], inv_ref[...])
        if then_upper:
            mid_ref[s] = value
            value = apply_inverse(value, (up_own_ref, up_oth_ref)[s][...])
        out_ref[s] = value


def pick(array, *at):
    tail = array.shape[len(at) :]
    return pl.BlockSpec((None,) * len(at) + tail, lambda i: tuple(at) + (0,) * len(tail))


def solve(parts, *operands, then_upper=False):
    shape = jax.ShapeDtypeStruct(parts.shape[1:], F32)
    whole = pl.BlockSpec(shape.shape, lambda i: (0, 0, 0))
    outs = 2 if then_upper else 1
    result = pl.pallas_call(
        lambda *refs: solve_kernel(then_upper, *refs),
        grid=(1,),
        out_shape=[shape] * outs,
        in_specs=[pl.BlockSpec(parts.shape, lambda i: (0, 0, 0, 0))] + [pick(*op) for op in operands],
        out_specs=[whole] * outs,
        compiler_params=pltpu.CompilerParams(vmem_limit_bytes=VMEM_LIMIT),
        cost_estimate=pl.CostEstimate(flops=1 << 24, bytes_accessed=1 << 20, transcendentals=0),
    )(parts, *[op[0] for op in operands])
    return result if then_upper else result[0]


def first_kernel(rhs_ref, inv_ref, out_ref):
    out_ref[...] = apply_inverse(rhs_ref[...], inv_ref[...])


def first_solve(rhs, inverse):
    return pl.pallas_call(
        first_kernel,
        grid=(1,),
        out_shape=jax.ShapeDtypeStruct(rhs.shape[1:], F32),
        in_specs=[pick(rhs, 0), pick(inverse, 0)],
        out_specs=pl.BlockSpec(rhs.shape[1:], lambda i: (0, 0)),
        compiler_params=pltpu.CompilerParams(vmem_limit_bytes=VMEM_LIMIT),
    )(rhs, inverse)


def body(rhs, l_inverse, u_inverse, l_tiles, l_source, l_target, l_rows, u_tiles, u_source, u_target, u_cols):
    rhs, l_inverse, u_inverse, l_tiles, l_source, l_target, l_rows, u_tiles, u_source, u_target, u_cols = (
        a[:, 0, 0] for a in (rhs, l_inverse, u_inverse, l_tiles, l_source, l_target, l_rows, u_tiles, u_source, u_target, u_cols)
    )
    levels, nrhs, width = rhs.shape
    steps = levels - 1
    tiles = l_tiles.shape[1]
    half = nrhs // 2
    prow = lax.axis_size("prow")
    pcol = lax.axis_size("pcol")
    parity = (lax.axis_index("prow") // 2) % 2
    pair = [(r, r ^ 2) for r in range(prow)]
    groups = [[4 * i + 2 * a + c for i in range(prow // 4) for c in range(2)] for a in range(2)]

    def swap(array):
        return lax.ppermute(array, "prow", pair)

    def halves(array):
        low, high = array[..., :half, :], array[..., half:, :]
        return jnp.where(parity == 0, low, high), jnp.where(parity == 0, high, low)

    def gather(value):
        got = lax.all_gather(value, "prow", axis=0, tiled=True, axis_index_groups=groups)
        return got.reshape(prow, half, width)

    def exchange(parts):
        return lax.all_to_all(parts, "pcol", 0, 0, tiled=True)

    mine, send = halves(first_solve(rhs, l_inverse))
    value = jnp.stack([mine, swap(send)])
    def packed(rows, source, target):
        return jnp.concatenate([rows, source[..., None], target[..., None]], axis=2)

    ints = jnp.stack([packed(l_rows, l_source, l_target), packed(u_cols, u_source, u_target)])
    ints = jnp.stack([ints, swap(ints)], axis=2).reshape(2 * steps, 2 * tiles, -1)
    rows = jnp.concatenate([ints[..., :-2], ints[..., :-2]], axis=2)
    raw = ints[..., -2].reshape(-1)
    source = (raw & ~3) + 2 * (raw & 1) + (((raw >> 1) & 1) ^ parity)
    target = ints[..., -1].reshape(-1)

    l_first = swap(l_tiles[:1])
    rhs_mine, rhs_send = halves(rhs[1:])
    rhs_oth = swap(rhs_send)
    l_inverse_oth = swap(l_inverse[1:])
    l_rest = swap(l_tiles[1:])
    u_inverse_oth = swap(u_inverse)
    u_oth = swap(u_tiles)

    forward = [value]
    result = None
    for level in range(1, levels):
        at = level - 1
        oth = (l_first, 0) if at == 0 else (l_rest, at - 1)
        parts = products(True, at * 2 * tiles, at, oth[1], source, target, rows, gather(value), l_tiles, oth[0])
        operands = [(rhs_mine, at), (rhs_oth, at), (l_inverse, level), (l_inverse_oth, at)]
        if level < levels - 1:
            value = solve(exchange(parts), *operands)
            forward.append(value)
        else:
            operands += [(u_inverse, level), (u_inverse_oth, level)]
            top, value = solve(exchange(parts), *operands, then_upper=True)
    result = [value]
    for level in range(levels - 2, -1, -1):
        offset = (steps + level) * 2 * tiles
        parts = products(False, offset, level, level, source, target, rows, gather(value), u_tiles, u_oth)
        start = forward[level]
        value = solve(exchange(parts), (start, 0), (start, 1), (u_inverse, level), (u_inverse_oth, level))
        result.append(value)
    result = jnp.stack(result[::-1])
    own, got = result[:, 0], swap(result[:, 1])
    solution = jnp.where(parity == 0, jnp.concatenate([own, got], axis=1), jnp.concatenate([got, own], axis=1))
    return solution[:, None, None]


def solution(mesh):
    spec = lambda tail: P(None, "prow", "pcol", *([None] * tail))
    in_specs = tuple(spec(n) for n in (2, 2, 2, 3, 1, 1, 2, 3, 1, 1, 2))
    return jax.shard_map(body, mesh=mesh, in_specs=in_specs, out_specs=spec(2), check_vma=False)
```

```python
import jax
import jax.numpy as jnp
from jax import lax
from jax.experimental import pallas as pl
from jax.experimental.pallas import tpu as pltpu
from jax.sharding import PartitionSpec as P

F32 = jnp.float32
BF16 = jnp.bfloat16
SMALL_VMEM = 12 * 1024 * 1024
LARGE_VMEM = 60 * 1024 * 1024
STEP_ROWS = 32


def dot_nt(a, b):
    return lax.dot_general(a, b, (((1,), (1,)), ((), ())), preferred_element_type=F32)


def dot_nn(a, b):
    return lax.dot_general(a, b, (((1,), (0,)), ((), ())), preferred_element_type=F32)


def split(x):
    high = x.astype(BF16)
    low = (x - high.astype(F32)).astype(BF16)
    return jnp.concatenate([high, low], axis=0)


def fold(x):
    half = x.shape[0] // 2
    return x[:half] + x[half:]


def apply_inverse(vectors, inverse):
    size = inverse.shape[0]
    out = fold(dot_nt(split(vectors), split(inverse)))
    return out[:, :size] + out[:, size:]


def structure_matrix(rows):
    positions = lax.broadcasted_iota(jnp.int32, (128, rows.shape[1]), 0).astype(rows.dtype)
    return jnp.where(positions == rows, 1.0, 0.0).astype(BF16)


def pick(array, *at):
    tail = array.shape[len(at) :]
    return pl.BlockSpec((None,) * len(at) + tail, lambda i: tuple(at) + (0,) * len(tail))


def rows_of(array, first, count, memory_space=None):
    assert first % count == 0
    return pl.BlockSpec((2, count, array.shape[2]), lambda i: (0, first // count, 0), memory_space=memory_space)


def scalars():
    return pl.BlockSpec(memory_space=pltpu.SMEM)


def call(kernel, outs, in_specs, operands, vmem=SMALL_VMEM, flops=1 << 24, scratch=(), grid=(1,)):
    return pl.pallas_call(
        kernel,
        grid=grid,
        out_shape=outs,
        in_specs=in_specs,
        out_specs=[pick(o) for o in outs],
        scratch_shapes=scratch,
        compiler_params=pltpu.CompilerParams(vmem_limit_bytes=vmem),
        cost_estimate=pl.CostEstimate(flops=flops, bytes_accessed=1 << 20, transcendentals=0),
    )(*operands)


def own_products_kernel(transposed, level, parity_ref, source_ref, target_ref, rows_ref, near_ref, far_ref, tiles_ref, out_ref, parts_ref):
    tiles = tiles_ref.shape[0]
    rows = rows_ref[...]
    rows = jnp.concatenate([rows, rows], axis=1)
    for first in range(0, tiles, 4):
        held = []
        for k in range(first, first + 4):
            source = source_ref[level, 0, 0, k]
            at = 2 * (source >> 2) + (source & 1)
            is_near = ((source >> 1) & 1) == parity_ref[0]
            block = split(jnp.where(is_near, near_ref[at], far_ref[at]))
            tile = split(tiles_ref[k])
            places = structure_matrix(rows[k : k + 1, :])
            if transposed:
                held.append((k, fold(dot_nt(block, tile)), places))
            else:
                held.append((k, dot_nn(block, places).astype(BF16), tile))
        for k, left, right in held:
            if transposed:
                parts_ref[k] = fold(dot_nt(split(left), right))
            else:
                parts_ref[k] = fold(dot_nn(left, right))
    out_ref[...] = jnp.zeros_like(out_ref)
    for k in range(tiles):
        out_ref[target_ref[level, 0, 0, k]] += parts_ref[k]


def own_products(transposed, level, parity, source, target, rows, near, far, tiles):
    count, (nrhs, width) = tiles.shape[3], near.shape[1:]
    outs = [jax.ShapeDtypeStruct((16, nrhs, width), F32)]
    in_specs = [scalars()] * 3 + [pick(rows, level, 0, 0), pick(near), pick(far), pick(tiles, level, 0, 0)]
    operands = (parity, source, target, rows, near, far, tiles)
    kernel = lambda *refs: own_products_kernel(transposed, level, *refs)
    return call(kernel, outs, in_specs, operands, flops=1 << 28, scratch=[pltpu.VMEM((count, nrhs, width), F32)])[0]


def products_kernel(transposed, tiles, height, at_ref, ints_ref, blocks_ref, tiles_ref, out_ref, parts_ref):
    first_lane = 0 if transposed else height
    rows = []
    for row in range(2):
        once = ints_ref[row, :tiles, first_lane : first_lane + height]
        rows.append(jnp.concatenate([once, once], axis=1))

    def scalar(row, kind, k):
        return at_ref[row, tiles + kind, first_lane + k].astype(jnp.int32)

    for first in range(0, 2 * tiles, 8):
        group = range(first, first + 8)
        held = []
        for t in group:
            row, k = divmod(t, tiles)
            at = scalar(row, 0, k)
            block = split(blocks_ref[(at & ~3) + 2 * (at & 1) + ((at >> 1) & 1)])
            tile = split(tiles_ref[row, k * height : (k + 1) * height, :])
            places = structure_matrix(rows[row][k : k + 1, :])
            if transposed:
                held.append((fold(dot_nt(block, tile)), places))
            else:
                held.append((dot_nn(block, places).astype(BF16), tile))
        for t, (left, right) in zip(group, held):
            if transposed:
                parts_ref[t] = fold(dot_nt(split(left), right))
            else:
                parts_ref[t] = fold(dot_nn(left, right))
    out_ref[...] = jnp.zeros_like(out_ref)
    for t in range(2 * tiles):
        row, k = divmod(t, tiles)
        out_ref[scalar(row, 1, k), row] += parts_ref[t]


def products(transposed, structure, structure_at, blocks, bundle, tiles, height):
    half, width = blocks.shape[1:]
    outs = [jax.ShapeDtypeStruct((16, 2, half, width), F32)]
    in_specs = [
        rows_of(structure, structure_at, STEP_ROWS, pltpu.SMEM),
        rows_of(structure, structure_at, STEP_ROWS),
        pick(blocks),
        rows_of(bundle, 0, tiles * height),
    ]
    scratch = [pltpu.VMEM((2 * tiles, half, width), F32)]
    kernel = lambda *refs: products_kernel(transposed, tiles, height, *refs)
    return call(kernel, outs, in_specs, (structure, structure, blocks, bundle), flops=1 << 28, scratch=scratch)[0]


def summed(parts_ref):
    total = parts_ref[0]
    for k in range(1, parts_ref.shape[0]):
        total = total + parts_ref[k]
    return total


def solve_kernel(mine, inverses, *refs):
    if mine:
        parity_ref, refs = refs[0], refs[1:]
    parts_ref, start_ref, inverse_refs, rest = refs[0], refs[1], refs[2 : 2 + inverses], refs[2 + inverses :]
    total = parts_ref[0]
    for k in range(1, parts_ref.shape[0]):
        total = total + parts_ref[k]
    if total.ndim == 2:
        rest[0][...] = apply_inverse(start_ref[...] - total, inverse_refs[0][...])
        return
    half = total.shape[1]
    stacked = len(rest[-1].shape) == 4
    for row in range(2):
        if mine:
            start = start_ref[row, pl.ds(pl.multiple_of(parity_ref[0] * half, half), half), :]
        else:
            start = start_ref[row]
        value = start - total[row]
        for k, inverse_ref in enumerate(inverse_refs):
            value = apply_inverse(value, inverse_ref[row])
            if stacked:
                rest[-1][0, row] = value
            else:
                rest[k][row] = value
    if stacked:
        for k, ref in enumerate(rest[:-1]):
            rest[-1][k + 1] = ref[...]


def first_forward(parts, rhs, inverse, level):
    outs = [jax.ShapeDtypeStruct(parts.shape[1:], F32)]
    in_specs = [pick(parts), pick(rhs, level, 0, 0), pick(inverse, level, 0, 0)]
    return call(lambda *refs: solve_kernel(False, 1, *refs), outs, in_specs, (parts, rhs, inverse))[0]


def pair_solve(parity, parts, start, inverses, higher=()):
    _, _, half, width = parts.shape
    shape = jax.ShapeDtypeStruct(parts.shape[1:], F32)
    whole = isinstance(start, tuple)
    in_specs, operands = ([scalars()], [parity]) if whole else ([], [])
    in_specs += [pick(parts), rows_of(*start, 2 * half) if whole else pick(start)]
    operands += [parts, start[0] if whole else start]
    in_specs += [rows_of(*inverse, width) for inverse in inverses] + [pick(h) for h in higher]
    operands += [inverse[0] for inverse in inverses] + list(higher)
    outs = [shape] * len(inverses)
    if higher:
        outs = [jax.ShapeDtypeStruct((len(higher) + 1,) + shape.shape, F32)]
    return call(lambda *refs: solve_kernel(whole, len(inverses), *refs), outs, in_specs, operands)


def first_kernel(rhs_ref, inv_ref, *rest):
    ints_refs, (out_ref, structure_ref) = rest[:6], rest[6:]
    out_ref[...] = apply_inverse(rhs_ref[...], inv_ref[...])
    structure_ref[...] = jnp.zeros_like(structure_ref)
    for factor in range(2):
        rows_ref, source_ref, target_ref = ints_refs[3 * factor : 3 * factor + 3]
        steps, _, _, tiles, height = rows_ref.shape
        lanes = factor * height
        for k in range(steps):
            at = k * STEP_ROWS
            structure_ref[at : at + tiles, lanes : lanes + height] = rows_ref[k, 0, 0].astype(F32)
            structure_ref[at + tiles : at + tiles + 1, lanes : lanes + tiles] = source_ref[k, 0].astype(F32)
            structure_ref[at + tiles + 1 : at + tiles + 2, lanes : lanes + tiles] = target_ref[k, 0].astype(F32)


def first_solve(rhs, inverse, *ints):
    nrhs, width = rhs.shape[3:]
    steps = ints[0].shape[0]
    outs = [jax.ShapeDtypeStruct((rows, width), F32) for rows in (nrhs, steps * STEP_ROWS)]
    in_specs = [pick(rhs, 0, 0, 0), pick(inverse, 0, 0, 0)] + [pick(a) for a in ints]
    return call(first_kernel, outs, in_specs, (rhs, inverse, *ints), vmem=LARGE_VMEM)


def bundles_kernel(plans, *refs):
    sems = refs[-1]
    outs = refs[-1 - len(plans) : -1]
    copies = []
    for plan, out_ref in zip(plans, outs):
        first = 0
        for operand, level, rows in plan:
            src = refs[operand] if level is None else refs[operand].at[level]
            copies.append(pltpu.make_async_copy(src, out_ref.at[pl.ds(first, rows)], sems.at[len(copies)]))
            copies[-1].start()
            first += rows
    for copy in copies:
        copy.wait()


def build_bundles(arrays, held):
    plans = [[(at, level, arrays[at].shape[-2]) for at, level in items] for items in held]
    width = arrays[0].shape[-1]
    outs = [jax.ShapeDtypeStruct((sum(rows for _, _, rows in plan), width), F32) for plan in plans]
    scratch = [pltpu.SemaphoreType.DMA((sum(len(plan) for plan in plans),))]
    in_specs = [pl.BlockSpec(memory_space=pl.ANY)] * len(arrays)
    return call(lambda *refs: bundles_kernel(plans, *refs), outs, in_specs, arrays, vmem=LARGE_VMEM, scratch=scratch)


def last_kernel(parity_ref, both_ref, out_ref):
    parity = parity_ref[0]
    half = both_ref.shape[3]
    for z in range(2):
        for k in range(both_ref.shape[1]):
            out_ref[k, 0, 0, z * half : (z + 1) * half, :] = both_ref[z, k, parity]


def last_step(parity, both):
    _, levels, _, half, width = both.shape
    outs = [jax.ShapeDtypeStruct((levels, 1, 1, 2 * half, width), F32)]
    return call(last_kernel, outs, [scalars(), pick(both)], (parity, both))[0]


def body(rhs, l_inverse, u_inverse, l_tiles, l_source, l_target, l_rows, u_tiles, u_source, u_target, u_cols):
    ints = (l_rows, l_source, l_target, u_cols, u_source, u_target)
    levels, nrhs, width = rhs.shape[0], rhs.shape[3], rhs.shape[4]
    half = nrhs // 2
    tiles, height = l_tiles.shape[3:5]
    prow = lax.axis_size("prow")
    at = (lax.axis_index("prow") >> 1) & 1
    parity = at.reshape(1).astype(jnp.int32)
    pairs = [[4 * i + c, 4 * i + 2 + c] for i in range(prow // 4) for c in range(2)]
    groups = [[4 * i + 2 * a + c for i in range(prow // 4) for c in range(2)] for a in range(2)]
    onward = [(r, (r + 2 if r % 2 == 0 else r - 2) % prow) for r in range(prow)]

    def both(array):
        return lax.all_gather(array, "prow", axis=0, tiled=False, axis_index_groups=pairs)

    def gather(value):
        return lax.all_gather(value, "prow", axis=0, tiled=True, axis_index_groups=groups)

    def exchange(parts):
        return lax.all_to_all(parts, "pcol", 0, 0, tiled=True)

    def after(array, earlier):
        return lax.optimization_barrier((array, earlier))

    first, structure = first_solve(rhs, l_inverse, *ints)
    near = gather(first[None])
    raw = (l_tiles, u_tiles, l_inverse, u_inverse, rhs)
    raw = [a.reshape(a.shape[0], -1, width) for a in raw] + [structure, first]
    near, *raw = lax.optimization_barrier((near, *raw))
    far = lax.ppermute(near, "prow", onward)
    held = [
        [(0, 1), (2, 2), (4, 2), (5, None)],
        [(0, 2), (2, 3), (3, 3), (4, 3)],
        [(1, 2), (3, 2)],
        [(1, 1), (3, 1)],
        [(1, 0), (3, 0), (6, None)],
    ]
    bundles = list(build_bundles(raw, held))
    parts = own_products(True, 0, parity, l_source, l_target, l_rows, near, far, l_tiles)
    in_tiles = tiles * height
    shared = [both(bundles[0])]
    second = first_forward(exchange(parts), rhs, l_inverse, 1)
    bundles[1], second = after(bundles[1], second)
    shared.append(both(bundles[1]))
    value = lax.dynamic_slice(both(second), (0, at * half, 0), (2, half, width))
    forward = [None, value]
    result = []
    for step, level in enumerate([2, 3, 2, 1, 0]):
        is_forward = step < 2
        mine = shared[step]
        if step:
            mine, value = after(mine, value)
        blocks = gather(value).reshape(prow, half, width)
        if step + 2 < len(bundles):
            later, blocks = after(bundles[step + 2], blocks)
            shared.append(both(later))
        structure_at = in_tiles + width + nrhs + (level - 1 if is_forward else level) * STEP_ROWS
        parts = products(is_forward, shared[0], structure_at, blocks, mine, tiles, height)
        got = exchange(parts)
        if step == 0:
            (value,) = pair_solve(parity, got, (mine, in_tiles + width), [(mine, in_tiles)])
            forward.append(value)
            continue
        if step == 1:
            inverses = [(mine, in_tiles), (mine, in_tiles + width)]
            _, value = pair_solve(parity, got, (mine, in_tiles + 2 * width), inverses)
        elif level > 0:
            (value,) = pair_solve(parity, got, forward[level], [(mine, in_tiles)])
        else:
            (value,) = pair_solve(parity, got, (mine, in_tiles + width), [(mine, in_tiles)], result[::-1])
        result.append(value)
    return last_step(parity, both(value))


def solution(mesh):
    spec = lambda tail: P(None, "prow", "pcol", *([None] * tail))
    in_specs = tuple(spec(n) for n in (2, 2, 2, 3, 1, 1, 2, 3, 1, 1, 2))
    return jax.shard_map(body, mesh=mesh, in_specs=in_specs, out_specs=spec(2), check_vma=False)
```

```python
import jax
import jax.numpy as jnp
from jax import lax
from jax.experimental import pallas as pl
from jax.experimental.pallas import tpu as pltpu
from jax.sharding import PartitionSpec as P

F32 = jnp.float32
BF16 = jnp.bfloat16
SMALL_VMEM = 12 * 1024 * 1024
LARGE_VMEM = 60 * 1024 * 1024
STEP_ROWS = 32


def dot_nt(a, b):
    return lax.dot_general(a, b, (((1,), (1,)), ((), ())), preferred_element_type=F32)


def dot_nn(a, b):
    return lax.dot_general(a, b, (((1,), (0,)), ((), ())), preferred_element_type=F32)


def split(x):
    high = x.astype(BF16)
    low = (x - high.astype(F32)).astype(BF16)
    return jnp.concatenate([high, low], axis=0)


def fold(x):
    half = x.shape[0] // 2
    return x[:half] + x[half:]


def apply_inverse(vectors, inverse):
    size = inverse.shape[0]
    out = fold(dot_nt(split(vectors), split(inverse)))
    return out[:, :size] + out[:, size:]


def structure_matrix(rows):
    positions = lax.broadcasted_iota(jnp.int32, (128, rows.shape[1]), 0).astype(rows.dtype)
    return jnp.where(positions == rows, 1.0, 0.0).astype(BF16)


def pick(array, *at):
    tail = array.shape[len(at) :]
    return pl.BlockSpec((None,) * len(at) + tail, lambda i: tuple(at) + (0,) * len(tail))


def rows_of(array, first, count, memory_space=None):
    assert first % count == 0
    return pl.BlockSpec((2, count, array.shape[2]), lambda i: (0, first // count, 0), memory_space=memory_space)


def scalars():
    return pl.BlockSpec(memory_space=pltpu.SMEM)


def call(kernel, outs, in_specs, operands, vmem=SMALL_VMEM, flops=1 << 24, scratch=(), grid=(1,)):
    return pl.pallas_call(
        kernel,
        grid=grid,
        out_shape=outs,
        in_specs=in_specs,
        out_specs=[pick(o) for o in outs],
        scratch_shapes=scratch,
        compiler_params=pltpu.CompilerParams(vmem_limit_bytes=vmem),
        cost_estimate=pl.CostEstimate(flops=flops, bytes_accessed=1 << 20, transcendentals=0),
    )(*operands)


def own_products_kernel(transposed, level, parity_ref, source_ref, target_ref, rows_ref, near_ref, far_ref, tiles_ref, out_ref, parts_ref):
    tiles = tiles_ref.shape[0]
    rows = rows_ref[...]
    rows = jnp.concatenate([rows, rows], axis=1)
    for first in range(0, tiles, 4):
        held = []
        for k in range(first, first + 4):
            source = source_ref[level, 0, 0, k]
            at = 2 * (source >> 2) + (source & 1)
            is_near = ((source >> 1) & 1) == parity_ref[0]
            block = split(jnp.where(is_near, near_ref[at], far_ref[at]))
            tile = split(tiles_ref[k])
            places = structure_matrix(rows[k : k + 1, :])
            if transposed:
                held.append((k, fold(dot_nt(block, tile)), places))
            else:
                held.append((k, dot_nn(block, places).astype(BF16), tile))
        for k, left, right in held:
            if transposed:
                parts_ref[k] = fold(dot_nt(split(left), right))
            else:
                parts_ref[k] = fold(dot_nn(left, right))
    out_ref[...] = jnp.zeros_like(out_ref)
    for k in range(tiles):
        out_ref[target_ref[level, 0, 0, k]] += parts_ref[k]


def own_products(transposed, level, parity, source, target, rows, near, far, tiles):
    count, (nrhs, width) = tiles.shape[3], near.shape[1:]
    outs = [jax.ShapeDtypeStruct((16, nrhs, width), F32)]
    in_specs = [scalars()] * 3 + [pick(rows, level, 0, 0), pick(near), pick(far), pick(tiles, level, 0, 0)]
    operands = (parity, source, target, rows, near, far, tiles)
    kernel = lambda *refs: own_products_kernel(transposed, level, *refs)
    return call(kernel, outs, in_specs, operands, flops=1 << 28, scratch=[pltpu.VMEM((count, nrhs, width), F32)])[0]


def products_kernel(transposed, tiles, height, at_ref, ints_ref, blocks_ref, tiles_ref, out_ref, parts_ref):
    first_lane = 0 if transposed else height
    rows = []
    for row in range(2):
        once = ints_ref[row, :tiles, first_lane : first_lane + height]
        rows.append(jnp.concatenate([once, once], axis=1))

    def scalar(row, kind, k):
        return at_ref[row, tiles + kind, first_lane + k].astype(jnp.int32)

    for first in range(0, 2 * tiles, 8):
        group = range(first, first + 8)
        held = []
        for t in group:
            row, k = divmod(t, tiles)
            at = scalar(row, 0, k)
            block = split(blocks_ref[(at & ~3) + 2 * (at & 1) + ((at >> 1) & 1)])
            tile = split(tiles_ref[row, k * height : (k + 1) * height, :])
            places = structure_matrix(rows[row][k : k + 1, :])
            if transposed:
                held.append((fold(dot_nt(block, tile)), places))
            else:
                held.append((dot_nn(block, places).astype(BF16), tile))
        for t, (left, right) in zip(group, held):
            if transposed:
                parts_ref[t] = fold(dot_nt(split(left), right))
            else:
                parts_ref[t] = fold(dot_nn(left, right))
    out_ref[...] = jnp.zeros_like(out_ref)
    for t in range(2 * tiles):
        row, k = divmod(t, tiles)
        out_ref[scalar(row, 1, k), row] += parts_ref[t]


def products(transposed, structure, structure_at, blocks, bundle, tiles, height):
    half, width = blocks.shape[1:]
    outs = [jax.ShapeDtypeStruct((16, 2, half, width), F32)]
    in_specs = [
        rows_of(structure, structure_at, STEP_ROWS, pltpu.SMEM),
        rows_of(structure, structure_at, STEP_ROWS),
        pick(blocks),
        rows_of(bundle, 0, tiles * height),
    ]
    scratch = [pltpu.VMEM((2 * tiles, half, width), F32)]
    kernel = lambda *refs: products_kernel(transposed, tiles, height, *refs)
    return call(kernel, outs, in_specs, (structure, structure, blocks, bundle), flops=1 << 28, scratch=scratch)[0]


def summed(parts_ref):
    total = parts_ref[0]
    for k in range(1, parts_ref.shape[0]):
        total = total + parts_ref[k]
    return total


def solve_kernel(mine, inverses, *refs):
    if mine:
        parity_ref, refs = refs[0], refs[1:]
    parts_ref, start_ref, inverse_refs, rest = refs[0], refs[1], refs[2 : 2 + inverses], refs[2 + inverses :]
    total = parts_ref[0]
    for k in range(1, parts_ref.shape[0]):
        total = total + parts_ref[k]
    if total.ndim == 2:
        rest[0][...] = apply_inverse(start_ref[...] - total, inverse_refs[0][...])
        return
    half = total.shape[1]
    stacked = len(rest[-1].shape) == 4
    for row in range(2):
        if mine:
            start = start_ref[row, pl.ds(pl.multiple_of(parity_ref[0] * half, half), half), :]
        else:
            start = start_ref[row]
        value = start - total[row]
        for k, inverse_ref in enumerate(inverse_refs):
            value = apply_inverse(value, inverse_ref[row])
            if stacked:
                rest[-1][0, row] = value
            else:
                rest[k][row] = value
    if stacked:
        for k, ref in enumerate(rest[:-1]):
            rest[-1][k + 1] = ref[...]


def first_forward(parts, rhs, inverse, level):
    outs = [jax.ShapeDtypeStruct(parts.shape[1:], F32)]
    in_specs = [pick(parts), pick(rhs, level, 0, 0), pick(inverse, level, 0, 0)]
    return call(lambda *refs: solve_kernel(False, 1, *refs), outs, in_specs, (parts, rhs, inverse))[0]


def pair_solve(parity, parts, start, inverses, higher=()):
    _, _, half, width = parts.shape
    shape = jax.ShapeDtypeStruct(parts.shape[1:], F32)
    whole = isinstance(start, tuple)
    in_specs, operands = ([scalars()], [parity]) if whole else ([], [])
    in_specs += [pick(parts), rows_of(*start, 2 * half) if whole else pick(start)]
    operands += [parts, start[0] if whole else start]
    in_specs += [rows_of(*inverse, width) for inverse in inverses] + [pick(h) for h in higher]
    operands += [inverse[0] for inverse in inverses] + list(higher)
    outs = [shape] * len(inverses)
    if higher:
        outs = [jax.ShapeDtypeStruct((len(higher) + 1,) + shape.shape, F32)]
    return call(lambda *refs: solve_kernel(whole, len(inverses), *refs), outs, in_specs, operands)


def first_kernel(rhs_ref, inv_ref, *rest):
    ints_refs, (out_ref, structure_ref) = rest[:6], rest[6:]
    out_ref[...] = apply_inverse(rhs_ref[...], inv_ref[...])
    structure_ref[...] = jnp.zeros_like(structure_ref)
    for factor in range(2):
        rows_ref, source_ref, target_ref = ints_refs[3 * factor : 3 * factor + 3]
        steps, _, _, tiles, height = rows_ref.shape
        lanes = factor * height
        for k in range(steps):
            at = k * STEP_ROWS
            structure_ref[at : at + tiles, lanes : lanes + height] = rows_ref[k, 0, 0].astype(F32)
            structure_ref[at + tiles : at + tiles + 1, lanes : lanes + tiles] = source_ref[k, 0].astype(F32)
            structure_ref[at + tiles + 1 : at + tiles + 2, lanes : lanes + tiles] = target_ref[k, 0].astype(F32)


def first_solve(rhs, inverse, *ints):
    nrhs, width = rhs.shape[3:]
    steps = ints[0].shape[0]
    outs = [jax.ShapeDtypeStruct((rows, width), F32) for rows in (nrhs, steps * STEP_ROWS)]
    in_specs = [pick(rhs, 0, 0, 0), pick(inverse, 0, 0, 0)] + [pick(a) for a in ints]
    return call(first_kernel, outs, in_specs, (rhs, inverse, *ints), vmem=LARGE_VMEM)


def bundles_kernel(plans, *refs):
    sems = refs[-1]
    outs = refs[-1 - len(plans) : -1]
    copies = []
    for plan, out_ref in zip(plans, outs):
        first = 0
        for operand, level, rows in plan:
            src = refs[operand] if level is None else refs[operand].at[level]
            copies.append(pltpu.make_async_copy(src, out_ref.at[pl.ds(first, rows)], sems.at[len(copies)]))
            copies[-1].start()
            first += rows
    for copy in copies:
        copy.wait()


def build_bundles(arrays, held):
    plans = [[(at, level, arrays[at].shape[-2]) for at, level in items] for items in held]
    width = arrays[0].shape[-1]
    outs = [jax.ShapeDtypeStruct((sum(rows for _, _, rows in plan), width), F32) for plan in plans]
    scratch = [pltpu.SemaphoreType.DMA((sum(len(plan) for plan in plans),))]
    in_specs = [pl.BlockSpec(memory_space=pl.ANY)] * len(arrays)
    return call(lambda *refs: bundles_kernel(plans, *refs), outs, in_specs, arrays, vmem=LARGE_VMEM, scratch=scratch)


def last_kernel(parity_ref, both_ref, out_ref):
    parity = parity_ref[0]
    half = both_ref.shape[3]
    for z in range(2):
        for k in range(both_ref.shape[1]):
            out_ref[k, 0, 0, z * half : (z + 1) * half, :] = both_ref[z, k, parity]


def last_step(parity, both):
    _, levels, _, half, width = both.shape
    outs = [jax.ShapeDtypeStruct((levels, 1, 1, 2 * half, width), F32)]
    return call(last_kernel, outs, [scalars(), pick(both)], (parity, both))[0]


def body(rhs, l_inverse, u_inverse, l_tiles, l_source, l_target, l_rows, u_tiles, u_source, u_target, u_cols):
    ints = (l_rows, l_source, l_target, u_cols, u_source, u_target)
    levels, nrhs, width = rhs.shape[0], rhs.shape[3], rhs.shape[4]
    half = nrhs // 2
    tiles, height = l_tiles.shape[3:5]
    prow = lax.axis_size("prow")
    at = (lax.axis_index("prow") >> 1) & 1
    parity = at.reshape(1).astype(jnp.int32)
    pairs = [[4 * i + c, 4 * i + 2 + c] for i in range(prow // 4) for c in range(2)]
    groups = [[4 * i + 2 * a + c for i in range(prow // 4) for c in range(2)] for a in range(2)]
    onward = [(r, (r + 2 if r % 2 == 0 else r - 2) % prow) for r in range(prow)]

    def both(array):
        return lax.all_gather(array, "prow", axis=0, tiled=False, axis_index_groups=pairs)

    def gather(value):
        return lax.all_gather(value, "prow", axis=0, tiled=True, axis_index_groups=groups)

    def exchange(parts):
        return lax.all_to_all(parts, "pcol", 0, 0, tiled=True)

    def after(array, earlier):
        return lax.optimization_barrier((array, earlier))

    first, structure = first_solve(rhs, l_inverse, *ints)
    near = gather(first[None])
    raw = (l_tiles, u_tiles, l_inverse, u_inverse, rhs)
    raw = [a.reshape(a.shape[0], -1, width) for a in raw] + [structure, first]
    near, *raw = lax.optimization_barrier((near, *raw))
    far = lax.ppermute(near, "prow", onward)
    held = [
        [(0, 1), (2, 2), (4, 2), (5, None)],
        [(0, 2), (2, 3), (3, 3), (4, 3)],
        [(1, 2), (3, 2)],
        [(1, 1), (3, 1)],
        [(1, 0), (3, 0), (6, None)],
    ]
    bundles = list(build_bundles(raw, held[:1])) + list(build_bundles(raw, held[1:]))
    near, *bundles[1:] = lax.optimization_barrier((near, *bundles[1:]))
    parts = own_products(True, 0, parity, l_source, l_target, l_rows, near, far, l_tiles)
    in_tiles = tiles * height
    shared = [both(bundles[0])]
    second = first_forward(exchange(parts), rhs, l_inverse, 1)
    bundles[1], second = after(bundles[1], second)
    shared.append(both(bundles[1]))
    value = lax.dynamic_slice(both(second), (0, at * half, 0), (2, half, width))
    forward = [None, value]
    result = []
    for step, level in enumerate([2, 3, 2, 1, 0]):
        is_forward = step < 2
        mine = shared[step]
        if step + 2 < len(bundles):
            later, value = after(bundles[step + 2], value)
            shared.append(both(later))
        blocks = gather(value).reshape(prow, half, width)
        structure_at = in_tiles + width + nrhs + (level - 1 if is_forward else level) * STEP_ROWS
        parts = products(is_forward, shared[0], structure_at, blocks, mine, tiles, height)
        got = exchange(parts)
        if step == 0:
            (value,) = pair_solve(parity, got, (mine, in_tiles + width), [(mine, in_tiles)])
            forward.append(value)
            continue
        if step == 1:
            inverses = [(mine, in_tiles), (mine, in_tiles + width)]
            _, value = pair_solve(parity, got, (mine, in_tiles + 2 * width), inverses)
        elif level > 0:
            (value,) = pair_solve(parity, got, forward[level], [(mine, in_tiles)])
        else:
            (value,) = pair_solve(parity, got, (mine, in_tiles + width), [(mine, in_tiles)], result[::-1])
        result.append(value)
    return last_step(parity, both(value))


def solution(mesh):
    spec = lambda tail: P(None, "prow", "pcol", *([None] * tail))
    in_specs = tuple(spec(n) for n in (2, 2, 2, 3, 1, 1, 2, 3, 1, 1, 2))
    return jax.shard_map(body, mesh=mesh, in_specs=in_specs, out_specs=spec(2), check_vma=False)
```

```python
import jax
import jax.numpy as jnp
from jax import lax
from jax.experimental import pallas as pl
from jax.experimental.pallas import tpu as pltpu
from jax.sharding import PartitionSpec as P

F32 = jnp.float32
BF16 = jnp.bfloat16
SMALL_VMEM = 12 * 1024 * 1024
LARGE_VMEM = 60 * 1024 * 1024
STEP_ROWS = 32


def dot_nt(a, b):
    return lax.dot_general(a, b, (((1,), (1,)), ((), ())), preferred_element_type=F32)


def dot_nn(a, b):
    return lax.dot_general(a, b, (((1,), (0,)), ((), ())), preferred_element_type=F32)


def split(x):
    high = x.astype(BF16)
    low = (x - high.astype(F32)).astype(BF16)
    return jnp.concatenate([high, low], axis=0)


def fold(x):
    half = x.shape[0] // 2
    return x[:half] + x[half:]


def apply_inverse(vectors, inverse):
    size = inverse.shape[0]
    out = fold(dot_nt(split(vectors), split(inverse)))
    return out[:, :size] + out[:, size:]


def structure_matrix(rows):
    positions = lax.broadcasted_iota(jnp.int32, (128, rows.shape[1]), 0).astype(rows.dtype)
    return jnp.where(positions == rows, 1.0, 0.0).astype(BF16)


def pick(array, *at):
    tail = array.shape[len(at) :]
    return pl.BlockSpec((None,) * len(at) + tail, lambda i: tuple(at) + (0,) * len(tail))


def rows_of(array, first, count, memory_space=None):
    assert first % count == 0
    return pl.BlockSpec((2, count, array.shape[2]), lambda i: (0, first // count, 0), memory_space=memory_space)


def scalars():
    return pl.BlockSpec(memory_space=pltpu.SMEM)


def call(kernel, outs, in_specs, operands, vmem=SMALL_VMEM, flops=1 << 24, scratch=(), grid=(1,)):
    return pl.pallas_call(
        kernel,
        grid=grid,
        out_shape=outs,
        in_specs=in_specs,
        out_specs=[pick(o) for o in outs],
        scratch_shapes=scratch,
        compiler_params=pltpu.CompilerParams(vmem_limit_bytes=vmem),
        cost_estimate=pl.CostEstimate(flops=flops, bytes_accessed=1 << 20, transcendentals=0),
    )(*operands)


def own_products_kernel(transposed, level, parity_ref, source_ref, target_ref, rows_ref, near_ref, far_ref, tiles_ref, out_ref, parts_ref):
    tiles = tiles_ref.shape[0]
    rows = rows_ref[...]
    rows = jnp.concatenate([rows, rows], axis=1)
    for first in range(0, tiles, 8):
        held = []
        for k in range(first, first + 8):
            source = source_ref[level, 0, 0, k]
            at = 2 * (source >> 2) + (source & 1)
            is_near = ((source >> 1) & 1) == parity_ref[0]
            block = split(jnp.where(is_near, near_ref[at], far_ref[at]))
            tile = split(tiles_ref[k])
            places = structure_matrix(rows[k : k + 1, :])
            if transposed:
                held.append((k, fold(dot_nt(block, tile)), places))
            else:
                held.append((k, dot_nn(block, places).astype(BF16), tile))
        for k, left, right in held:
            if transposed:
                parts_ref[k] = fold(dot_nt(split(left), right))
            else:
                parts_ref[k] = fold(dot_nn(left, right))
    out_ref[...] = jnp.zeros_like(out_ref)
    for k in range(tiles):
        out_ref[target_ref[level, 0, 0, k]] += parts_ref[k]


def own_products(transposed, level, parity, source, target, rows, near, far, tiles):
    count, (nrhs, width) = tiles.shape[3], near.shape[1:]
    outs = [jax.ShapeDtypeStruct((16, nrhs, width), F32)]
    in_specs = [scalars()] * 3 + [pick(rows, level, 0, 0), pick(near), pick(far), pick(tiles, level, 0, 0)]
    operands = (parity, source, target, rows, near, far, tiles)
    kernel = lambda *refs: own_products_kernel(transposed, level, *refs)
    return call(kernel, outs, in_specs, operands, flops=1 << 28, scratch=[pltpu.VMEM((count, nrhs, width), F32)])[0]


def products_kernel(transposed, tiles, height, at_ref, ints_ref, blocks_ref, tiles_ref, out_ref, parts_ref):
    first_lane = 0 if transposed else height
    rows = []
    for row in range(2):
        once = ints_ref[row, :tiles, first_lane : first_lane + height]
        rows.append(jnp.concatenate([once, once], axis=1))

    def scalar(row, kind, k):
        return at_ref[row, tiles + kind, first_lane + k].astype(jnp.int32)

    for first in range(0, 2 * tiles, 16):
        group = range(first, first + 16)
        held = []
        for t in group:
            row, k = divmod(t, tiles)
            at = scalar(row, 0, k)
            block = split(blocks_ref[(at & ~3) + 2 * (at & 1) + ((at >> 1) & 1)])
            tile = split(tiles_ref[row, k * height : (k + 1) * height, :])
            places = structure_matrix(rows[row][k : k + 1, :])
            if transposed:
                held.append((fold(dot_nt(block, tile)), places))
            else:
                held.append((dot_nn(block, places).astype(BF16), tile))
        for t, (left, right) in zip(group, held):
            if transposed:
                parts_ref[t] = fold(dot_nt(split(left), right))
            else:
                parts_ref[t] = fold(dot_nn(left, right))
    out_ref[...] = jnp.zeros_like(out_ref)
    for t in range(2 * tiles):
        row, k = divmod(t, tiles)
        out_ref[scalar(row, 1, k), row] += parts_ref[t]


def products(transposed, structure, structure_at, blocks, bundle, tiles, height):
    half, width = blocks.shape[1:]
    outs = [jax.ShapeDtypeStruct((16, 2, half, width), F32)]
    in_specs = [
        rows_of(structure, structure_at, STEP_ROWS, pltpu.SMEM),
        rows_of(structure, structure_at, STEP_ROWS),
        pick(blocks),
        rows_of(bundle, 0, tiles * height),
    ]
    scratch = [pltpu.VMEM((2 * tiles, half, width), F32)]
    kernel = lambda *refs: products_kernel(transposed, tiles, height, *refs)
    return call(kernel, outs, in_specs, (structure, structure, blocks, bundle), flops=1 << 28, scratch=scratch)[0]


def summed(parts_ref):
    total = parts_ref[0]
    for k in range(1, parts_ref.shape[0]):
        total = total + parts_ref[k]
    return total


def solve_kernel(mine, inverses, *refs):
    if mine:
        parity_ref, refs = refs[0], refs[1:]
    parts_ref, start_ref, inverse_refs, rest = refs[0], refs[1], refs[2 : 2 + inverses], refs[2 + inverses :]
    total = parts_ref[0]
    for k in range(1, parts_ref.shape[0]):
        total = total + parts_ref[k]
    if total.ndim == 2:
        rest[0][...] = apply_inverse(start_ref[...] - total, inverse_refs[0][...])
        return
    half = total.shape[1]
    stacked = len(rest[-1].shape) == 4
    for row in range(2):
        if mine:
            start = start_ref[row, pl.ds(pl.multiple_of(parity_ref[0] * half, half), half), :]
        else:
            start = start_ref[row]
        value = start - total[row]
        for k, inverse_ref in enumerate(inverse_refs):
            value = apply_inverse(value, inverse_ref[row])
            if stacked:
                rest[-1][0, row] = value
            else:
                rest[k][row] = value
    if stacked:
        for k, ref in enumerate(rest[:-1]):
            rest[-1][k + 1] = ref[...]


def first_forward(parts, rhs, inverse, level):
    outs = [jax.ShapeDtypeStruct(parts.shape[1:], F32)]
    in_specs = [pick(parts), pick(rhs, level, 0, 0), pick(inverse, level, 0, 0)]
    return call(lambda *refs: solve_kernel(False, 1, *refs), outs, in_specs, (parts, rhs, inverse))[0]


def pair_solve(parity, parts, start, inverses, higher=()):
    _, _, half, width = parts.shape
    shape = jax.ShapeDtypeStruct(parts.shape[1:], F32)
    whole = isinstance(start, tuple)
    in_specs, operands = ([scalars()], [parity]) if whole else ([], [])
    in_specs += [pick(parts), rows_of(*start, 2 * half) if whole else pick(start)]
    operands += [parts, start[0] if whole else start]
    in_specs += [rows_of(*inverse, width) for inverse in inverses] + [pick(h) for h in higher]
    operands += [inverse[0] for inverse in inverses] + list(higher)
    outs = [shape] * len(inverses)
    if higher:
        outs = [jax.ShapeDtypeStruct((len(higher) + 1,) + shape.shape, F32)]
    return call(lambda *refs: solve_kernel(whole, len(inverses), *refs), outs, in_specs, operands)


def first_kernel(rhs_ref, inv_ref, *rest):
    ints_refs, (out_ref, structure_ref) = rest[:6], rest[6:]
    out_ref[...] = apply_inverse(rhs_ref[...], inv_ref[...])
    structure_ref[...] = jnp.zeros_like(structure_ref)
    for factor in range(2):
        rows_ref, source_ref, target_ref = ints_refs[3 * factor : 3 * factor + 3]
        steps, _, _, tiles, height = rows_ref.shape
        lanes = factor * height
        for k in range(steps):
            at = k * STEP_ROWS
            structure_ref[at : at + tiles, lanes : lanes + height] = rows_ref[k, 0, 0].astype(F32)
            structure_ref[at + tiles : at + tiles + 1, lanes : lanes + tiles] = source_ref[k, 0].astype(F32)
            structure_ref[at + tiles + 1 : at + tiles + 2, lanes : lanes + tiles] = target_ref[k, 0].astype(F32)


def first_solve(rhs, inverse, *ints):
    nrhs, width = rhs.shape[3:]
    steps = ints[0].shape[0]
    outs = [jax.ShapeDtypeStruct((rows, width), F32) for rows in (nrhs, steps * STEP_ROWS)]
    in_specs = [pick(rhs, 0, 0, 0), pick(inverse, 0, 0, 0)] + [pick(a) for a in ints]
    return call(first_kernel, outs, in_specs, (rhs, inverse, *ints), vmem=LARGE_VMEM)


def bundles_kernel(plans, *refs):
    sems = refs[-1]
    outs = refs[-1 - len(plans) : -1]
    copies = []
    for plan, out_ref in zip(plans, outs):
        first = 0
        for operand, level, rows in plan:
            src = refs[operand] if level is None else refs[operand].at[level]
            copies.append(pltpu.make_async_copy(src, out_ref.at[pl.ds(first, rows)], sems.at[len(copies)]))
            copies[-1].start()
            first += rows
    for copy in copies:
        copy.wait()


def build_bundles(arrays, held):
    plans = [[(at, level, arrays[at].shape[-2]) for at, level in items] for items in held]
    width = arrays[0].shape[-1]
    outs = [jax.ShapeDtypeStruct((sum(rows for _, _, rows in plan), width), F32) for plan in plans]
    scratch = [pltpu.SemaphoreType.DMA((sum(len(plan) for plan in plans),))]
    in_specs = [pl.BlockSpec(memory_space=pl.ANY)] * len(arrays)
    return call(lambda *refs: bundles_kernel(plans, *refs), outs, in_specs, arrays, vmem=LARGE_VMEM, scratch=scratch)


def last_kernel(parity_ref, both_ref, out_ref):
    parity = parity_ref[0]
    half = both_ref.shape[3]
    for z in range(2):
        for k in range(both_ref.shape[1]):
            out_ref[k, 0, 0, z * half : (z + 1) * half, :] = both_ref[z, k, parity]


def last_step(parity, both):
    _, levels, _, half, width = both.shape
    outs = [jax.ShapeDtypeStruct((levels, 1, 1, 2 * half, width), F32)]
    return call(last_kernel, outs, [scalars(), pick(both)], (parity, both))[0]


def body(rhs, l_inverse, u_inverse, l_tiles, l_source, l_target, l_rows, u_tiles, u_source, u_target, u_cols):
    ints = (l_rows, l_source, l_target, u_cols, u_source, u_target)
    levels, nrhs, width = rhs.shape[0], rhs.shape[3], rhs.shape[4]
    half = nrhs // 2
    tiles, height = l_tiles.shape[3:5]
    prow = lax.axis_size("prow")
    at = (lax.axis_index("prow") >> 1) & 1
    parity = at.reshape(1).astype(jnp.int32)
    pairs = [[4 * i + c, 4 * i + 2 + c] for i in range(prow // 4) for c in range(2)]
    groups = [[4 * i + 2 * a + c for i in range(prow // 4) for c in range(2)] for a in range(2)]
    onward = [(r, (r + 2 if r % 2 == 0 else r - 2) % prow) for r in range(prow)]

    def both(array):
        return lax.all_gather(array, "prow", axis=0, tiled=False, axis_index_groups=pairs)

    def gather(value):
        return lax.all_gather(value, "prow", axis=0, tiled=True, axis_index_groups=groups)

    def exchange(parts):
        return lax.all_to_all(parts, "pcol", 0, 0, tiled=True)

    def after(array, earlier):
        return lax.optimization_barrier((array, earlier))

    first, structure = first_solve(rhs, l_inverse, *ints)
    near = gather(first[None])
    raw = (l_tiles, u_tiles, l_inverse, u_inverse, rhs)
    raw = [a.reshape(a.shape[0], -1, width) for a in raw] + [structure, first]
    near, *raw = lax.optimization_barrier((near, *raw))
    far = lax.ppermute(near, "prow", onward)
    held = [
        [(0, 1), (2, 2), (4, 2), (5, None)],
        [(0, 2), (2, 3), (3, 3), (4, 3)],
        [(1, 2), (3, 2)],
        [(1, 1), (3, 1)],
        [(1, 0), (3, 0), (6, None)],
    ]
    bundles = list(build_bundles(raw, held[:1])) + list(build_bundles(raw, held[1:]))
    near, *bundles[1:] = lax.optimization_barrier((near, *bundles[1:]))
    parts = own_products(True, 0, parity, l_source, l_target, l_rows, near, far, l_tiles)
    in_tiles = tiles * height
    shared = [both(bundles[0])]
    second = first_forward(exchange(parts), rhs, l_inverse, 1)
    bundles[1], second = after(bundles[1], second)
    shared.append(both(bundles[1]))
    value = lax.dynamic_slice(both(second), (0, at * half, 0), (2, half, width))
    forward = [None, value]
    result = []
    for step, level in enumerate([2, 3, 2, 1, 0]):
        is_forward = step < 2
        mine = shared[step]
        if step + 2 < len(bundles):
            later, value = after(bundles[step + 2], value)
            shared.append(both(later))
        blocks = gather(value).reshape(prow, half, width)
        structure_at = in_tiles + width + nrhs + (level - 1 if is_forward else level) * STEP_ROWS
        parts = products(is_forward, shared[0], structure_at, blocks, mine, tiles, height)
        got = exchange(parts)
        if step == 0:
            (value,) = pair_solve(parity, got, (mine, in_tiles + width), [(mine, in_tiles)])
            forward.append(value)
            continue
        if step == 1:
            inverses = [(mine, in_tiles), (mine, in_tiles + width)]
            _, value = pair_solve(parity, got, (mine, in_tiles + 2 * width), inverses)
        elif level > 0:
            (value,) = pair_solve(parity, got, forward[level], [(mine, in_tiles)])
        else:
            (value,) = pair_solve(parity, got, (mine, in_tiles + width), [(mine, in_tiles)], result[::-1])
        result.append(value)
    return last_step(parity, both(value))


def solution(mesh):
    spec = lambda tail: P(None, "prow", "pcol", *([None] * tail))
    in_specs = tuple(spec(n) for n in (2, 2, 2, 3, 1, 1, 2, 3, 1, 1, 2))
    return jax.shard_map(body, mesh=mesh, in_specs=in_specs, out_specs=spec(2), check_vma=False)
```

```python
import jax
import jax.numpy as jnp
from jax import lax
from jax.experimental import pallas as pl
from jax.experimental.pallas import tpu as pltpu
from jax.sharding import PartitionSpec as P

F32 = jnp.float32
BF16 = jnp.bfloat16
SMALL_VMEM = 12 * 1024 * 1024
LARGE_VMEM = 60 * 1024 * 1024
STEP_ROWS = 32


def dot_nt(a, b):
    return lax.dot_general(a, b, (((1,), (1,)), ((), ())), preferred_element_type=F32)


def dot_nn(a, b):
    return lax.dot_general(a, b, (((1,), (0,)), ((), ())), preferred_element_type=F32)


def split(x):
    high = x.astype(BF16)
    low = (x - high.astype(F32)).astype(BF16)
    return jnp.concatenate([high, low], axis=0)


def fold(x):
    half = x.shape[0] // 2
    return x[:half] + x[half:]


def apply_inverse(vectors, inverse):
    size = inverse.shape[0]
    out = fold(dot_nt(split(vectors), split(inverse)))
    return out[:, :size] + out[:, size:]


def structure_matrix(rows):
    positions = lax.broadcasted_iota(jnp.int32, (128, rows.shape[1]), 0).astype(rows.dtype)
    return jnp.where(positions == rows, 1.0, 0.0).astype(BF16)


def pick(array, *at):
    tail = array.shape[len(at) :]
    return pl.BlockSpec((None,) * len(at) + tail, lambda i: tuple(at) + (0,) * len(tail))


def rows_of(array, first, count, memory_space=None):
    assert first % count == 0
    return pl.BlockSpec((2, count, array.shape[2]), lambda i: (0, first // count, 0), memory_space=memory_space)


def scalars():
    return pl.BlockSpec(memory_space=pltpu.SMEM)


def call(kernel, outs, in_specs, operands, vmem=SMALL_VMEM, flops=1 << 24, scratch=(), grid=(1,)):
    return pl.pallas_call(
        kernel,
        grid=grid,
        out_shape=outs,
        in_specs=in_specs,
        out_specs=[pick(o) for o in outs],
        scratch_shapes=scratch,
        compiler_params=pltpu.CompilerParams(vmem_limit_bytes=vmem),
        cost_estimate=pl.CostEstimate(flops=flops, bytes_accessed=1 << 20, transcendentals=0),
    )(*operands)


def own_products_kernel(transposed, level, parity_ref, source_ref, target_ref, rows_ref, near_ref, far_ref, tiles_ref, out_ref, parts_ref):
    tiles = tiles_ref.shape[0]
    rows = rows_ref[...]
    rows = jnp.concatenate([rows, rows], axis=1)
    for first in range(0, tiles, 16):
        held = []
        for k in range(first, first + 16):
            source = source_ref[level, 0, 0, k]
            at = 2 * (source >> 2) + (source & 1)
            is_near = ((source >> 1) & 1) == parity_ref[0]
            block = split(jnp.where(is_near, near_ref[at], far_ref[at]))
            tile = split(tiles_ref[k])
            places = structure_matrix(rows[k : k + 1, :])
            if transposed:
                held.append((k, fold(dot_nt(block, tile)), places))
            else:
                held.append((k, dot_nn(block, places).astype(BF16), tile))
        for k, left, right in held:
            if transposed:
                parts_ref[k] = fold(dot_nt(split(left), right))
            else:
                parts_ref[k] = fold(dot_nn(left, right))
    out_ref[...] = jnp.zeros_like(out_ref)
    for k in range(tiles):
        out_ref[target_ref[level, 0, 0, k]] += parts_ref[k]


def own_products(transposed, level, parity, source, target, rows, near, far, tiles):
    count, (nrhs, width) = tiles.shape[3], near.shape[1:]
    outs = [jax.ShapeDtypeStruct((16, nrhs, width), F32)]
    in_specs = [scalars()] * 3 + [pick(rows, level, 0, 0), pick(near), pick(far), pick(tiles, level, 0, 0)]
    operands = (parity, source, target, rows, near, far, tiles)
    kernel = lambda *refs: own_products_kernel(transposed, level, *refs)
    return call(kernel, outs, in_specs, operands, flops=1 << 28, scratch=[pltpu.VMEM((count, nrhs, width), F32)])[0]


def products_kernel(transposed, tiles, height, at_ref, ints_ref, blocks_ref, tiles_ref, out_ref, parts_ref):
    first_lane = 0 if transposed else height
    rows = []
    for row in range(2):
        once = ints_ref[row, :tiles, first_lane : first_lane + height]
        rows.append(jnp.concatenate([once, once], axis=1))

    def scalar(row, kind, k):
        return at_ref[row, tiles + kind, first_lane + k].astype(jnp.int32)

    for first in range(0, 2 * tiles, 32):
        group = range(first, first + 32)
        held = []
        for t in group:
            row, k = divmod(t, tiles)
            at = scalar(row, 0, k)
            block = split(blocks_ref[(at & ~3) + 2 * (at & 1) + ((at >> 1) & 1)])
            tile = split(tiles_ref[row, k * height : (k + 1) * height, :])
            places = structure_matrix(rows[row][k : k + 1, :])
            if transposed:
                held.append((fold(dot_nt(block, tile)), places))
            else:
                held.append((dot_nn(block, places).astype(BF16), tile))
        for t, (left, right) in zip(group, held):
            if transposed:
                parts_ref[t] = fold(dot_nt(split(left), right))
            else:
                parts_ref[t] = fold(dot_nn(left, right))
    out_ref[...] = jnp.zeros_like(out_ref)
    for t in range(2 * tiles):
        row, k = divmod(t, tiles)
        out_ref[scalar(row, 1, k), row] += parts_ref[t]


def products(transposed, structure, structure_at, blocks, bundle, tiles, height):
    half, width = blocks.shape[1:]
    outs = [jax.ShapeDtypeStruct((16, 2, half, width), F32)]
    in_specs = [
        rows_of(structure, structure_at, STEP_ROWS, pltpu.SMEM),
        rows_of(structure, structure_at, STEP_ROWS),
        pick(blocks),
        rows_of(bundle, 0, tiles * height),
    ]
    scratch = [pltpu.VMEM((2 * tiles, half, width), F32)]
    kernel = lambda *refs: products_kernel(transposed, tiles, height, *refs)
    return call(kernel, outs, in_specs, (structure, structure, blocks, bundle), flops=1 << 28, scratch=scratch)[0]


def summed(parts_ref):
    total = parts_ref[0]
    for k in range(1, parts_ref.shape[0]):
        total = total + parts_ref[k]
    return total


def solve_kernel(mine, inverses, *refs):
    if mine:
        parity_ref, refs = refs[0], refs[1:]
    parts_ref, start_ref, inverse_refs, rest = refs[0], refs[1], refs[2 : 2 + inverses], refs[2 + inverses :]
    total = parts_ref[0]
    for k in range(1, parts_ref.shape[0]):
        total = total + parts_ref[k]
    if total.ndim == 2:
        rest[0][...] = apply_inverse(start_ref[...] - total, inverse_refs[0][...])
        return
    half = total.shape[1]
    stacked = len(rest[-1].shape) == 4
    for row in range(2):
        if mine:
            start = start_ref[row, pl.ds(pl.multiple_of(parity_ref[0] * half, half), half), :]
        else:
            start = start_ref[row]
        value = start - total[row]
        for k, inverse_ref in enumerate(inverse_refs):
            value = apply_inverse(value, inverse_ref[row])
            if stacked:
                rest[-1][0, row] = value
            else:
                rest[k][row] = value
    if stacked:
        for k, ref in enumerate(rest[:-1]):
            rest[-1][k + 1] = ref[...]


def first_forward(parts, rhs, inverse, level):
    outs = [jax.ShapeDtypeStruct(parts.shape[1:], F32)]
    in_specs = [pick(parts), pick(rhs, level, 0, 0), pick(inverse, level, 0, 0)]
    return call(lambda *refs: solve_kernel(False, 1, *refs), outs, in_specs, (parts, rhs, inverse))[0]


def pair_solve(parity, parts, start, inverses, higher=()):
    _, _, half, width = parts.shape
    shape = jax.ShapeDtypeStruct(parts.shape[1:], F32)
    whole = isinstance(start, tuple)
    in_specs, operands = ([scalars()], [parity]) if whole else ([], [])
    in_specs += [pick(parts), rows_of(*start, 2 * half) if whole else pick(start)]
    operands += [parts, start[0] if whole else start]
    in_specs += [rows_of(*inverse, width) for inverse in inverses] + [pick(h) for h in higher]
    operands += [inverse[0] for inverse in inverses] + list(higher)
    outs = [shape] * len(inverses)
    if higher:
        outs = [jax.ShapeDtypeStruct((len(higher) + 1,) + shape.shape, F32)]
    return call(lambda *refs: solve_kernel(whole, len(inverses), *refs), outs, in_specs, operands)


def first_kernel(rhs_ref, inv_ref, *rest):
    ints_refs, (out_ref, structure_ref) = rest[:6], rest[6:]
    out_ref[...] = apply_inverse(rhs_ref[...], inv_ref[...])
    structure_ref[...] = jnp.zeros_like(structure_ref)
    for factor in range(2):
        rows_ref, source_ref, target_ref = ints_refs[3 * factor : 3 * factor + 3]
        steps, _, _, tiles, height = rows_ref.shape
        lanes = factor * height
        for k in range(steps):
            at = k * STEP_ROWS
            structure_ref[at : at + tiles, lanes : lanes + height] = rows_ref[k, 0, 0].astype(F32)
            structure_ref[at + tiles : at + tiles + 1, lanes : lanes + tiles] = source_ref[k, 0].astype(F32)
            structure_ref[at + tiles + 1 : at + tiles + 2, lanes : lanes + tiles] = target_ref[k, 0].astype(F32)


def first_solve(rhs, inverse, *ints):
    nrhs, width = rhs.shape[3:]
    steps = ints[0].shape[0]
    outs = [jax.ShapeDtypeStruct((rows, width), F32) for rows in (nrhs, steps * STEP_ROWS)]
    in_specs = [pick(rhs, 0, 0, 0), pick(inverse, 0, 0, 0)] + [pick(a) for a in ints]
    return call(first_kernel, outs, in_specs, (rhs, inverse, *ints), vmem=LARGE_VMEM)


def bundles_kernel(plans, *refs):
    sems = refs[-1]
    outs = refs[-1 - len(plans) : -1]
    copies = []
    for plan, out_ref in zip(plans, outs):
        first = 0
        for operand, level, rows in plan:
            src = refs[operand] if level is None else refs[operand].at[level]
            copies.append(pltpu.make_async_copy(src, out_ref.at[pl.ds(first, rows)], sems.at[len(copies)]))
            copies[-1].start()
            first += rows
    for copy in copies:
        copy.wait()


def build_bundles(arrays, held):
    plans = [[(at, level, arrays[at].shape[-2]) for at, level in items] for items in held]
    width = arrays[0].shape[-1]
    outs = [jax.ShapeDtypeStruct((sum(rows for _, _, rows in plan), width), F32) for plan in plans]
    scratch = [pltpu.SemaphoreType.DMA((sum(len(plan) for plan in plans),))]
    in_specs = [pl.BlockSpec(memory_space=pl.ANY)] * len(arrays)
    return call(lambda *refs: bundles_kernel(plans, *refs), outs, in_specs, arrays, vmem=LARGE_VMEM, scratch=scratch)


def last_kernel(parity_ref, both_ref, out_ref):
    parity = parity_ref[0]
    half = both_ref.shape[3]
    for z in range(2):
        for k in range(both_ref.shape[1]):
            out_ref[k, 0, 0, z * half : (z + 1) * half, :] = both_ref[z, k, parity]


def last_step(parity, both):
    _, levels, _, half, width = both.shape
    outs = [jax.ShapeDtypeStruct((levels, 1, 1, 2 * half, width), F32)]
    return call(last_kernel, outs, [scalars(), pick(both)], (parity, both))[0]


def body(rhs, l_inverse, u_inverse, l_tiles, l_source, l_target, l_rows, u_tiles, u_source, u_target, u_cols):
    ints = (l_rows, l_source, l_target, u_cols, u_source, u_target)
    levels, nrhs, width = rhs.shape[0], rhs.shape[3], rhs.shape[4]
    half = nrhs // 2
    tiles, height = l_tiles.shape[3:5]
    prow = lax.axis_size("prow")
    at = (lax.axis_index("prow") >> 1) & 1
    parity = at.reshape(1).astype(jnp.int32)
    pairs = [[4 * i + c, 4 * i + 2 + c] for i in range(prow // 4) for c in range(2)]
    groups = [[4 * i + 2 * a + c for i in range(prow // 4) for c in range(2)] for a in range(2)]
    onward = [(r, (r + 2 if r % 2 == 0 else r - 2) % prow) for r in range(prow)]

    def both(array):
        return lax.all_gather(array, "prow", axis=0, tiled=False, axis_index_groups=pairs)

    def gather(value):
        return lax.all_gather(value, "prow", axis=0, tiled=True, axis_index_groups=groups)

    def exchange(parts):
        return lax.all_to_all(parts, "pcol", 0, 0, tiled=True)

    def after(array, earlier):
        return lax.optimization_barrier((array, earlier))

    first, structure = first_solve(rhs, l_inverse, *ints)
    near = gather(first[None])
    raw = (l_tiles, u_tiles, l_inverse, u_inverse, rhs)
    raw = [a.reshape(a.shape[0], -1, width) for a in raw] + [structure, first]
    near, *raw = lax.optimization_barrier((near, *raw))
    far = lax.ppermute(near, "prow", onward)
    held = [
        [(0, 1), (2, 2), (4, 2), (5, None)],
        [(0, 2), (2, 3), (3, 3), (4, 3)],
        [(1, 2), (3, 2)],
        [(1, 1), (3, 1)],
        [(1, 0), (3, 0), (6, None)],
    ]
    bundles = list(build_bundles(raw, held[:1])) + list(build_bundles(raw, held[1:]))
    near, *bundles[1:] = lax.optimization_barrier((near, *bundles[1:]))
    parts = own_products(True, 0, parity, l_source, l_target, l_rows, near, far, l_tiles)
    in_tiles = tiles * height
    shared = [both(bundles[0])]
    second = first_forward(exchange(parts), rhs, l_inverse, 1)
    bundles[1], second = after(bundles[1], second)
    shared.append(both(bundles[1]))
    value = lax.dynamic_slice(both(second), (0, at * half, 0), (2, half, width))
    forward = [None, value]
    result = []
    for step, level in enumerate([2, 3, 2, 1, 0]):
        is_forward = step < 2
        mine = shared[step]
        if step + 2 < len(bundles):
            later, value = after(bundles[step + 2], value)
            shared.append(both(later))
        blocks = gather(value).reshape(prow, half, width)
        structure_at = in_tiles + width + nrhs + (level - 1 if is_forward else level) * STEP_ROWS
        parts = products(is_forward, shared[0], structure_at, blocks, mine, tiles, height)
        got = exchange(parts)
        if step == 0:
            (value,) = pair_solve(parity, got, (mine, in_tiles + width), [(mine, in_tiles)])
            forward.append(value)
            continue
        if step == 1:
            inverses = [(mine, in_tiles), (mine, in_tiles + width)]
            _, value = pair_solve(parity, got, (mine, in_tiles + 2 * width), inverses)
        elif level > 0:
            (value,) = pair_solve(parity, got, forward[level], [(mine, in_tiles)])
        else:
            (value,) = pair_solve(parity, got, (mine, in_tiles + width), [(mine, in_tiles)], result[::-1])
        result.append(value)
    return last_step(parity, both(value))


def solution(mesh):
    spec = lambda tail: P(None, "prow", "pcol", *([None] * tail))
    in_specs = tuple(spec(n) for n in (2, 2, 2, 3, 1, 1, 2, 3, 1, 1, 2))
    return jax.shard_map(body, mesh=mesh, in_specs=in_specs, out_specs=spec(2), check_vma=False)
```
